32 devices in a mesh: tm: 4 (over y, core), chan: 8 (over z, x).
Axes of the slice: x: 2, y: 2, z: 4, core: 2. Of those that a mesh axis runs over, the one named last changes fastest.
Arguments:
- voltages: bfloat16 [1024, 274432], P('chan', 'tm'), may hold values from -6 to 6
- taper_weights: float32 [4, 1024], replicated, may hold values from -1 to 1
Outputs:
- visibilities: bfloat16 [256, 2, 1024, 1024], P(('tm', 'chan'))
The draws below stay inside these ranges and needn't reach their ends.
All inputs are finite; a program needn't handle non-finite values.
Results may differ from the reference program's by a relative error of at most 0.0071.
Values may be sent and summed in bfloat16 or wider, within the bound.
A program may use at most 192 MiB of HBM per device.

```python
import math
import jax
import jax.numpy as jnp
from jax import lax

NI = 1024
L = 1024
CH = 256
TAPS = 4
SPEC_DEV = 64
NSPEC = 256
N_TM = 4


def shard_levels(rng, shape, split, low, high):
    factor_of, own = 1.0, jax.random.fold_in(rng, 6)
    for dim, blocks in split:
        heights = jnp.exp(jax.random.uniform(jax.random.fold_in(own, dim), (blocks,), jnp.float32, low / len(split), high / len(split)))
        factor_of = factor_of * jnp.repeat(heights, shape[dim] // blocks).reshape([-1 if axis == dim else 1 for axis in range(len(shape))])
    return factor_of


def centred(rng, extent, deviation, bound, cuts=(), kind=jnp.bfloat16):
    drawn = deviation * jax.random.normal(rng, extent, jnp.float32)
    if cuts:
        drawn = drawn * shard_levels(rng, extent, cuts, -0.22, 0.18)
    return jnp.clip(drawn, -bound, bound).astype(kind)


def setup_inputs(seed: int = 0) -> dict:
    keys = jax.random.split(jax.random.key(seed), 3)
    voltages = centred(keys[0], (NI, N_TM * (SPEC_DEV + TAPS - 1) * L), 1.0, 6.0, ((0, 8), (1, 4)))
    taper_weights = jnp.clip(jax.random.uniform(keys[1], (TAPS, L), jnp.float32, -1.0, 1.0), -1.0, 1.0)
    return {"voltages": voltages, "taper_weights": taper_weights}


def dft_table(length, channels):
    sample_idx = jnp.arange(length, dtype=jnp.int32)[:, None]
    column = jnp.arange(2 * channels, dtype=jnp.int32)[None, :]
    freq = column // 2 + channels // 2
    phase = ((sample_idx * freq) % length).astype(jnp.float32) * (2.0 * math.pi / length)
    values = jnp.where(column % 2 == 0, jnp.cos(phase), -jnp.sin(phase))
    return values.astype(jnp.bfloat16)


def correlate_one(spec):
    real_part = spec[0].astype(jnp.float32)
    imag_part = spec[1].astype(jnp.float32)
    left_rows = jnp.concatenate([real_part, imag_part], axis=1)
    other_rows = jnp.concatenate([imag_part, -real_part], axis=1)
    stacked = jnp.concatenate([left_rows, other_rows], axis=0)
    product = jnp.dot(stacked, left_rows.T)
    return (product.reshape(2, NI, NI) * (1.0 / NSPEC)).astype(jnp.bfloat16)


def reference(voltages, taper_weights):
    frame_count = SPEC_DEV + TAPS - 1
    table = dft_table(L, CH).astype(jnp.float32)
    pieces = []
    for tm_index in range(N_TM):
        segment = voltages[:, tm_index * frame_count * L:(tm_index + 1) * frame_count * L]
        frames = segment.reshape(NI, frame_count, L).astype(jnp.float32)
        filtered = taper_weights[0][None, None, :] * frames[:, 0:SPEC_DEV, :]
        for tap_index in range(1, TAPS):
            filtered = filtered + taper_weights[tap_index][None, None, :] * frames[:, tap_index:tap_index + SPEC_DEV, :]
        filtered = filtered.astype(jnp.bfloat16).astype(jnp.float32)
        spectra = jnp.einsum("isn,nc->cis", filtered, table) * (L ** -0.5)
        pieces.append(spectra.astype(jnp.bfloat16))
    spectra_all = jnp.concatenate(pieces, axis=2).reshape(CH, 2, NI, NSPEC)
    return lax.map(correlate_one, spectra_all)
```

```python
import functools
import math

import jax
import jax.numpy as jnp
import numpy as np
from jax import lax
from jax.experimental import pallas as pl
from jax.experimental.pallas import tpu as pltpu
from jax.sharding import PartitionSpec as P

L = 1024
CH = 256
TAPS = 4
SPEC_DEV = 64
MIB = 1024 * 1024
MESH = pl.DeviceIdType.MESH

STEP = 16
GROUP = 4


def table_rows():
    sample_idx = np.arange(L, dtype=np.int64)[None, :]
    column = np.arange(2 * CH, dtype=np.int64)[:, None]
    freq = column // 2 + CH // 2
    phase = (sample_idx * freq % L).astype(np.float32) * np.float32(2.0 * math.pi / L)
    phase = phase.astype(np.float64)
    values = np.where(column % 2 == 0, np.cos(phase), -np.sin(phase))
    values = values.astype(np.float32).astype(jnp.bfloat16).astype(np.float32)
    return (values * np.float32(L ** (-0.5))).astype(jnp.bfloat16)


def exchange_kernel(
    tm_n, chan_n, volt, taper, table, recv, vbuf, wide, filt, mid, send,
    hist_sem, load_sem, own_sem, send_sem, recv_sem,
):
    inputs = volt.shape[0]
    rows = 2 * CH // (tm_n * chan_n)
    steps = SPEC_DEV // STEP
    tm = lax.axis_index("tm")
    chan = lax.axis_index("chan")
    peers = tm_n * chan_n

    def load_hist():
        part = pl.ds(0, (TAPS - 1) * L)
        return pltpu.make_async_copy(volt.at[:, part], vbuf.at[:, part], hist_sem)

    def load_step(k):
        start = pl.multiple_of((TAPS - 1 + STEP * k) * L, L)
        part = pl.ds(start, STEP * L)
        return pltpu.make_async_copy(volt.at[:, part], vbuf.at[:, part], load_sem.at[k])

    load_hist().start()
    for k in range(steps):
        load_step(k).start()

    def partner(j):
        t = lax.rem(tm + j // chan_n, tm_n)
        c = lax.rem(chan + lax.rem(j, chan_n), chan_n)
        return t, c

    barrier = pltpu.get_barrier_semaphore()

    @pl.loop(1, peers)
    def _(j):
        t, c = partner(j)
        pl.semaphore_signal(barrier, inc=1, device_id=(t, c), device_id_type=MESH)

    for p in range(TAPS):
        wide[p] = jnp.broadcast_to(taper[p : p + 1, :], (16, L))

    load_hist().wait()
    lanes = 256

    @pl.loop(0, steps)
    def _(k):
        load_step(k).wait()

        @pl.loop(0, STEP // GROUP)
        def _(g):
            first = k * STEP + g * GROUP

            @pl.loop(0, inputs // 16)
            def _(b):
                r0 = pl.multiple_of(b * 16, 16)
                for n0 in range(0, L, lanes):
                    frames = []
                    for f in range(GROUP + TAPS - 1):
                        start = pl.multiple_of((first + f) * L + n0, 128)
                        frames.append(vbuf[pl.ds(r0, 16), pl.ds(start, lanes)].astype(jnp.float32))
                    weights = [wide[p, :, n0 : n0 + lanes] for p in range(TAPS)]
                    for s in range(GROUP):
                        total = weights[0] * frames[s]
                        for p in range(1, TAPS):
                            total = total + weights[p] * frames[s + p]
                        filt[s, pl.ds(r0, 16), n0 : n0 + lanes] = total.astype(jnp.bfloat16)

            for s in range(0, GROUP, 2):
                pair = filt[s : s + 2].reshape(2 * inputs, L)
                for h in range(0, 2 * CH, 256):
                    out = lax.dot_general(
                        table[h : h + 256], pair, (((1,), (1,)), ((), ())),
                        preferred_element_type=jnp.float32,
                    )
                    for q in range(2):
                        row = pl.multiple_of((g * GROUP + s + q) * (2 * CH), 2 * CH)
                        mid[pl.ds(row + h, 256), :] = out[:, q * inputs : (q + 1) * inputs]

        @pl.loop(0, 2 * CH // 8)
        def _(b):
            for u in range(8):
                col = b * 8 + u
                send[k, col] = mid[pl.ds(col, STEP, stride=2 * CH), :].astype(jnp.bfloat16)

        @pl.when(k == 0)
        def _():
            pl.semaphore_wait(barrier, peers - 1)

        where = pl.ds(pl.multiple_of(tm * SPEC_DEV + k * STEP, STEP), STEP)
        columns = pl.ds(pl.multiple_of(chan * inputs, inputs), inputs)

        @pl.loop(1, peers)
        def _(j):
            t, c = partner(j)
            pltpu.make_async_remote_copy(
                src_ref=send.at[k, pl.ds((t * chan_n + c) * rows, rows)],
                dst_ref=recv.at[:, where, columns],
                send_sem=send_sem.at[j],
                recv_sem=recv_sem.at[j],
                device_id=(t, c),
                device_id_type=MESH,
            ).start()

        pltpu.make_async_copy(
            send.at[k, pl.ds((tm * chan_n + chan) * rows, rows)],
            recv.at[:, where, columns],
            own_sem.at[k],
        ).start()

    where = pl.ds(pl.multiple_of(tm * SPEC_DEV, SPEC_DEV), SPEC_DEV)
    columns = pl.ds(pl.multiple_of(chan * inputs, inputs), inputs)

    @pl.loop(0, steps)
    def _(k):
        here = pl.ds(pl.multiple_of(tm * SPEC_DEV + k * STEP, STEP), STEP)
        pltpu.make_async_copy(
            send.at[k, pl.ds((tm * chan_n + chan) * rows, rows)],
            recv.at[:, here, columns],
            own_sem.at[k],
        ).wait()

    @pl.loop(1, peers)
    def _(j):
        t, c = partner(j)
        whole = pltpu.make_async_remote_copy(
            src_ref=recv.at[:, where, columns],
            dst_ref=recv.at[:, where, columns],
            send_sem=send_sem.at[j],
            recv_sem=recv_sem.at[j],
            device_id=(t, c),
            device_id_type=MESH,
        )
        whole.wait_send()
        whole.wait_recv()


def exchange(voltages, taper_weights, tm_n, chan_n):
    inputs = voltages.shape[0]
    rows = 2 * CH // (tm_n * chan_n)
    steps = SPEC_DEV // STEP
    peers = tm_n * chan_n
    table = jnp.asarray(table_rows())
    return pl.pallas_call(
        functools.partial(exchange_kernel, tm_n, chan_n),
        out_shape=jax.ShapeDtypeStruct((rows, SPEC_DEV * tm_n, inputs * chan_n), jnp.bfloat16),
        in_specs=[
            pl.BlockSpec(memory_space=pl.ANY),
            pl.BlockSpec(memory_space=pltpu.VMEM),
            pl.BlockSpec(memory_space=pltpu.VMEM),
        ],
        out_specs=pl.BlockSpec(memory_space=pl.ANY),
        scratch_shapes=[
            pltpu.VMEM(voltages.shape, jnp.bfloat16),
            pltpu.VMEM((TAPS, 16, L), jnp.float32),
            pltpu.VMEM((GROUP, inputs, L), jnp.bfloat16),
            pltpu.VMEM((STEP * 2 * CH, inputs), jnp.float32),
            pltpu.VMEM((steps, 2 * CH, STEP, inputs), jnp.bfloat16),
            pltpu.SemaphoreType.DMA,
            pltpu.SemaphoreType.DMA((steps,)),
            pltpu.SemaphoreType.DMA((steps,)),
            pltpu.SemaphoreType.DMA((peers,)),
            pltpu.SemaphoreType.DMA((peers,)),
        ],
        compiler_params=pltpu.CompilerParams(
            collective_id=0, has_side_effects=True, vmem_limit_bytes=48 * MIB
        ),
        cost_estimate=pl.CostEstimate(
            flops=4 * CH * L * inputs * SPEC_DEV, bytes_accessed=40 * MIB, transcendentals=0
        ),
    )(voltages, taper_weights, table)


def correlate_kernel(scale, spec, out, left):
    count = spec.shape[2]
    depth = spec.shape[1]
    tile = 256
    for m in range(0, count, tile):
        for r in range(2):
            turned = spec[r, :, m : m + tile].T
            left[0, m : m + tile, r * depth : (r + 1) * depth] = turned
            left[1, m : m + tile, (1 - r) * depth : (2 - r) * depth] = turned if r else -turned
    right = spec[...].reshape(2 * depth, count)
    for part in range(2):
        for m in range(0, count, tile):
            block = lax.dot_general(
                left[part, m : m + tile], right, (((1,), (0,)), ((), ())),
                preferred_element_type=jnp.float32,
            )
            out[0, part, m : m + tile] = (block * scale).astype(jnp.bfloat16)


def correlate_all(spectra):
    rows, depth, count = spectra.shape
    channels = rows // 2
    return pl.pallas_call(
        functools.partial(correlate_kernel, 1.0 / depth),
        grid=(channels,),
        out_shape=jax.ShapeDtypeStruct((channels, 2, count, count), jnp.bfloat16),
        in_specs=[pl.BlockSpec((2, depth, count), lambda c: (c, 0, 0))],
        out_specs=pl.BlockSpec((1, 2, count, count), lambda c: (c, 0, 0, 0)),
        scratch_shapes=[pltpu.VMEM((2, count, 2 * depth), jnp.bfloat16)],
        compiler_params=pltpu.CompilerParams(vmem_limit_bytes=48 * MIB),
        cost_estimate=pl.CostEstimate(
            flops=8 * channels * count * count * depth,
            bytes_accessed=channels * count * (4 * count + 4 * depth),
            transcendentals=0,
        ),
    )(spectra)


def dft_table(length, channels):
    sample_idx = jnp.arange(length, dtype=jnp.int32)[:, None]
    column = jnp.arange(2 * channels, dtype=jnp.int32)[None, :]
    freq = column // 2 + channels // 2
    phase = (sample_idx * freq % length).astype(jnp.float32) * (2.0 * math.pi / length)
    values = jnp.where(column % 2 == 0, jnp.cos(phase), -jnp.sin(phase))
    return values.astype(jnp.bfloat16)


def contract(rows, cols):
    return lax.dot_general(rows, cols, (((1,), (1,)), ((), ())), preferred_element_type=jnp.float32)


def correlate(spec):
    real_part = spec[0]
    imag_part = spec[1]
    left_rows = jnp.concatenate([real_part, imag_part], axis=1)
    other_rows = jnp.concatenate([imag_part, -real_part], axis=1)
    count = left_rows.shape[0]
    stacked = jnp.concatenate([left_rows, other_rows], axis=0)
    return contract(stacked, left_rows).reshape(2, count, count)


def shards_narrow(voltages, taper_weights, time_count, chan_count):
    inputs_here = voltages.shape[0]
    frame_count = SPEC_DEV + TAPS - 1
    frames = voltages.reshape(inputs_here, frame_count, L)
    filtered = taper_weights[0][None, None, :] * frames[:, 0:SPEC_DEV, :].astype(jnp.float32)
    for tap_index in range(1, TAPS):
        filtered = filtered + taper_weights[tap_index][None, None, :] * frames[
            :, tap_index : tap_index + SPEC_DEV, :
        ].astype(jnp.float32)
    filtered = filtered.astype(jnp.bfloat16)
    table = dft_table(L, CH)
    spectra = jnp.einsum(
        "isn,nc->cis", filtered, table, preferred_element_type=jnp.float32
    ) * L ** (-0.5)
    spectra = spectra.astype(jnp.bfloat16)
    per_owner = CH // (time_count * chan_count)
    spectra = spectra.reshape(time_count, chan_count, per_owner, 2, inputs_here, SPEC_DEV)
    scale = 1.0 / (SPEC_DEV * time_count)
    turned = lax.all_to_all(spectra, "tm", split_axis=0, concat_axis=5, tiled=True)
    piece = lax.all_to_all(turned, "chan", split_axis=1, concat_axis=4, tiled=True)
    flat = piece.reshape(piece.shape[2], 2, piece.shape[4], piece.shape[5])
    visibilities = lax.map(correlate, flat) * scale
    return visibilities.astype(jnp.bfloat16)


def shards(voltages, taper_weights):
    time_count = lax.axis_size("tm")
    chan_count = lax.axis_size("chan")
    if voltages.shape[0] % 128 == 0:
        return correlate_all(exchange(voltages, taper_weights, time_count, chan_count))
    return shards_narrow(voltages, taper_weights, time_count, chan_count)


def solution(mesh):
    placed = (P("chan", "tm"), P())
    return jax.shard_map(
        shards,
        mesh=mesh,
        in_specs=placed,
        out_specs=P(("tm", "chan"), None, None, None),
        check_vma=False,
    )
```

```python
import functools
import math

import jax
import jax.numpy as jnp
import numpy as np
from jax import lax
from jax.experimental import pallas as pl
from jax.experimental.pallas import tpu as pltpu
from jax.sharding import PartitionSpec as P

L = 1024
CH = 256
TAPS = 4
SPEC_DEV = 64
MIB = 1024 * 1024
MESH = pl.DeviceIdType.MESH

STEP = 16
GROUP = 4


def table_rows():
    sample_idx = np.arange(L, dtype=np.int64)[None, :]
    column = np.arange(2 * CH, dtype=np.int64)[:, None]
    freq = column // 2 + CH // 2
    phase = (sample_idx * freq % L).astype(np.float32) * np.float32(2.0 * math.pi / L)
    phase = phase.astype(np.float64)
    values = np.where(column % 2 == 0, np.cos(phase), -np.sin(phase))
    values = values.astype(np.float32).astype(jnp.bfloat16).astype(np.float32)
    return (values * np.float32(L ** (-0.5))).astype(jnp.bfloat16)


def exchange_kernel(
    tm_n, chan_n, volt, taper, table, recv, vbuf, wide, filt, mid, send,
    hist_sem, load_sem, own_sem, send_sem, recv_sem,
):
    inputs = volt.shape[0]
    rows = 2 * CH // (tm_n * chan_n)
    steps = SPEC_DEV // STEP
    tm = lax.axis_index("tm")
    chan = lax.axis_index("chan")
    peers = tm_n * chan_n
    me = tm * chan_n + chan

    def load_hist():
        part = pl.ds(0, (TAPS - 1) * L)
        return pltpu.make_async_copy(volt.at[:, part], vbuf.at[:, part], hist_sem)

    def load_step(k):
        start = pl.multiple_of((TAPS - 1 + STEP * k) * L, L)
        part = pl.ds(start, STEP * L)
        return pltpu.make_async_copy(volt.at[:, part], vbuf.at[:, part], load_sem.at[k])

    load_hist().start()
    for k in range(steps):
        load_step(k).start()

    def partner(j):
        t = lax.rem(tm + j // chan_n, tm_n)
        c = lax.rem(chan + lax.rem(j, chan_n), chan_n)
        return t, c

    barrier = pltpu.get_barrier_semaphore()

    @pl.loop(1, peers)
    def _(j):
        t, c = partner(j)
        pl.semaphore_signal(barrier, inc=1, device_id=(t, c), device_id_type=MESH)

    for p in range(TAPS):
        wide[p] = jnp.broadcast_to(taper[p : p + 1, :], (16, L))

    load_hist().wait()
    lanes = 256

    @pl.loop(0, steps)
    def _(k):
        load_step(k).wait()

        @pl.loop(0, STEP // GROUP)
        def _(g):
            first = k * STEP + g * GROUP

            @pl.loop(0, inputs // 16)
            def _(b):
                r0 = pl.multiple_of(b * 16, 16)
                for n0 in range(0, L, lanes):
                    frames = []
                    for f in range(GROUP + TAPS - 1):
                        start = pl.multiple_of((first + f) * L + n0, 128)
                        frames.append(vbuf[pl.ds(r0, 16), pl.ds(start, lanes)].astype(jnp.float32))
                    weights = [wide[p, :, n0 : n0 + lanes] for p in range(TAPS)]
                    for s in range(GROUP):
                        total = weights[0] * frames[s]
                        for p in range(1, TAPS):
                            total = total + weights[p] * frames[s + p]
                        filt[s, pl.ds(r0, 16), n0 : n0 + lanes] = total.astype(jnp.bfloat16)

            for s in range(0, GROUP, 2):
                pair = filt[s : s + 2].reshape(2 * inputs, L)
                for h in range(0, 2 * CH, 256):
                    out = lax.dot_general(
                        table[h : h + 256], pair, (((1,), (1,)), ((), ())),
                        preferred_element_type=jnp.float32,
                    )
                    for q in range(2):
                        row = pl.multiple_of((g * GROUP + s + q) * (2 * CH), 2 * CH)
                        mid[pl.ds(row + h, 256), :] = out[:, q * inputs : (q + 1) * inputs]

        @pl.loop(0, 2 * CH // 8)
        def _(b):
            for u in range(8):
                col = b * 8 + u
                send[k, col] = mid[pl.ds(col, STEP, stride=2 * CH), :].astype(jnp.bfloat16)

        @pl.when(k == 0)
        def _():
            pl.semaphore_wait(barrier, peers - 1)

        @pl.loop(0, peers)
        def _(n):
            far = lax.rem(lax.rem(n, chan_n) + 2 * tm + chan_n // 2, chan_n)
            j = n // chan_n * chan_n + far

            @pl.when(j != 0)
            def _():
                t, c = partner(j)
                pltpu.make_async_remote_copy(
                    src_ref=send.at[k, pl.ds((t * chan_n + c) * rows, rows)],
                    dst_ref=recv.at[me, k],
                    send_sem=send_sem.at[j],
                    recv_sem=recv_sem.at[j],
                    device_id=(t, c),
                    device_id_type=MESH,
                ).start()

        pltpu.make_async_copy(
            send.at[k, pl.ds(me * rows, rows)], recv.at[me, k], own_sem.at[k]
        ).start()

    @pl.loop(0, steps)
    def _(k):
        pltpu.make_async_copy(
            send.at[k, pl.ds(me * rows, rows)], recv.at[me, k], own_sem.at[k]
        ).wait()

    @pl.loop(1, peers)
    def _(j):
        t, c = partner(j)
        source = lax.rem(tm + tm_n - j // chan_n, tm_n) * chan_n + lax.rem(
            chan + chan_n - lax.rem(j, chan_n), chan_n
        )
        whole = pltpu.make_async_remote_copy(
            src_ref=recv.at[source],
            dst_ref=recv.at[source],
            send_sem=send_sem.at[j],
            recv_sem=recv_sem.at[j],
            device_id=(t, c),
            device_id_type=MESH,
        )
        whole.wait_send()
        whole.wait_recv()


def exchange(voltages, taper_weights, tm_n, chan_n):
    inputs = voltages.shape[0]
    rows = 2 * CH // (tm_n * chan_n)
    steps = SPEC_DEV // STEP
    peers = tm_n * chan_n
    table = jnp.asarray(table_rows())
    return pl.pallas_call(
        functools.partial(exchange_kernel, tm_n, chan_n),
        out_shape=jax.ShapeDtypeStruct((peers, steps, rows, STEP, inputs), jnp.bfloat16),
        in_specs=[
            pl.BlockSpec(memory_space=pl.ANY),
            pl.BlockSpec(memory_space=pltpu.VMEM),
            pl.BlockSpec(memory_space=pltpu.VMEM),
        ],
        out_specs=pl.BlockSpec(memory_space=pl.ANY),
        scratch_shapes=[
            pltpu.VMEM(voltages.shape, jnp.bfloat16),
            pltpu.VMEM((TAPS, 16, L), jnp.float32),
            pltpu.VMEM((GROUP, inputs, L), jnp.bfloat16),
            pltpu.VMEM((STEP * 2 * CH, inputs), jnp.float32),
            pltpu.VMEM((steps, 2 * CH, STEP, inputs), jnp.bfloat16),
            pltpu.SemaphoreType.DMA,
            pltpu.SemaphoreType.DMA((steps,)),
            pltpu.SemaphoreType.DMA((steps,)),
            pltpu.SemaphoreType.DMA((peers,)),
            pltpu.SemaphoreType.DMA((peers,)),
        ],
        compiler_params=pltpu.CompilerParams(
            collective_id=0, has_side_effects=True, vmem_limit_bytes=48 * MIB
        ),
        cost_estimate=pl.CostEstimate(
            flops=4 * CH * L * inputs * SPEC_DEV, bytes_accessed=40 * MIB, transcendentals=0
        ),
    )(voltages, taper_weights, table)


def correlate_kernel(chan_n, scale, spec, out, right):
    peers, steps, _, step, inputs = spec.shape
    depth = right.shape[0] // 2
    for p in range(peers):
        t, g = p // chan_n, p % chan_n
        for k in range(steps):
            for r in range(2):
                first = r * depth + (t * steps + k) * step
                right[first : first + step, g * inputs : (g + 1) * inputs] = spec[p, k, r]
    count = right.shape[1]
    tile = 256
    for m in range(0, count, tile):
        turned = right[:, m : m + tile].T
        other = jnp.concatenate([turned[:, depth:], -turned[:, :depth]], axis=1)
        both = jnp.concatenate([turned, other], axis=0)
        block = lax.dot_general(
            both, right[...], (((1,), (0,)), ((), ())), preferred_element_type=jnp.float32
        )
        block = (block * scale).astype(jnp.bfloat16)
        out[0, 0, m : m + tile] = block[:tile]
        out[0, 1, m : m + tile] = block[tile:]


def correlate_all(spectra, chan_n):
    peers, steps, rows, step, inputs = spectra.shape
    channels = rows // 2
    depth = peers // chan_n * steps * step
    count = chan_n * inputs
    return pl.pallas_call(
        functools.partial(correlate_kernel, chan_n, 1.0 / depth),
        grid=(channels,),
        out_shape=jax.ShapeDtypeStruct((channels, 2, count, count), jnp.bfloat16),
        in_specs=[pl.BlockSpec((peers, steps, 2, step, inputs), lambda c: (0, 0, c, 0, 0))],
        out_specs=pl.BlockSpec((1, 2, count, count), lambda c: (c, 0, 0, 0)),
        scratch_shapes=[pltpu.VMEM((2 * depth, count), jnp.bfloat16)],
        compiler_params=pltpu.CompilerParams(vmem_limit_bytes=48 * MIB),
        cost_estimate=pl.CostEstimate(
            flops=8 * channels * count * count * depth,
            bytes_accessed=channels * count * (4 * count + 4 * depth),
            transcendentals=0,
        ),
    )(spectra)


def dft_table(length, channels):
    sample_idx = jnp.arange(length, dtype=jnp.int32)[:, None]
    column = jnp.arange(2 * channels, dtype=jnp.int32)[None, :]
    freq = column // 2 + channels // 2
    phase = (sample_idx * freq % length).astype(jnp.float32) * (2.0 * math.pi / length)
    values = jnp.where(column % 2 == 0, jnp.cos(phase), -jnp.sin(phase))
    return values.astype(jnp.bfloat16)


def contract(rows, cols):
    return lax.dot_general(rows, cols, (((1,), (1,)), ((), ())), preferred_element_type=jnp.float32)


def correlate(spec):
    real_part = spec[0]
    imag_part = spec[1]
    left_rows = jnp.concatenate([real_part, imag_part], axis=1)
    other_rows = jnp.concatenate([imag_part, -real_part], axis=1)
    count = left_rows.shape[0]
    stacked = jnp.concatenate([left_rows, other_rows], axis=0)
    return contract(stacked, left_rows).reshape(2, count, count)


def shards_narrow(voltages, taper_weights, time_count, chan_count):
    inputs_here = voltages.shape[0]
    frame_count = SPEC_DEV + TAPS - 1
    frames = voltages.reshape(inputs_here, frame_count, L)
    filtered = taper_weights[0][None, None, :] * frames[:, 0:SPEC_DEV, :].astype(jnp.float32)
    for tap_index in range(1, TAPS):
        filtered = filtered + taper_weights[tap_index][None, None, :] * frames[
            :, tap_index : tap_index + SPEC_DEV, :
        ].astype(jnp.float32)
    filtered = filtered.astype(jnp.bfloat16)
    table = dft_table(L, CH)
    spectra = jnp.einsum(
        "isn,nc->cis", filtered, table, preferred_element_type=jnp.float32
    ) * L ** (-0.5)
    spectra = spectra.astype(jnp.bfloat16)
    per_owner = CH // (time_count * chan_count)
    spectra = spectra.reshape(time_count, chan_count, per_owner, 2, inputs_here, SPEC_DEV)
    scale = 1.0 / (SPEC_DEV * time_count)
    turned = lax.all_to_all(spectra, "tm", split_axis=0, concat_axis=5, tiled=True)
    piece = lax.all_to_all(turned, "chan", split_axis=1, concat_axis=4, tiled=True)
    flat = piece.reshape(piece.shape[2], 2, piece.shape[4], piece.shape[5])
    visibilities = lax.map(correlate, flat) * scale
    return visibilities.astype(jnp.bfloat16)


def shards(voltages, taper_weights):
    time_count = lax.axis_size("tm")
    chan_count = lax.axis_size("chan")
    if voltages.shape[0] % 128 == 0:
        return correlate_all(exchange(voltages, taper_weights, time_count, chan_count), chan_count)
    return shards_narrow(voltages, taper_weights, time_count, chan_count)


def solution(mesh):
    placed = (P("chan", "tm"), P())
    return jax.shard_map(
        shards,
        mesh=mesh,
        in_specs=placed,
        out_specs=P(("tm", "chan"), None, None, None),
        check_vma=False,
    )
```

```python
import functools
import math

import jax
import jax.numpy as jnp
import numpy as np
from jax import lax
from jax.experimental import pallas as pl
from jax.experimental.pallas import tpu as pltpu
from jax.sharding import PartitionSpec as P

L = 1024
CH = 256
TAPS = 4
SPEC_DEV = 64
MIB = 1024 * 1024
MESH = pl.DeviceIdType.MESH

STEP = 16
GROUP = 4


def table_rows():
    sample_idx = np.arange(L, dtype=np.int64)[None, :]
    column = np.arange(2 * CH, dtype=np.int64)[:, None]
    freq = column // 2 + CH // 2
    phase = (sample_idx * freq % L).astype(np.float32) * np.float32(2.0 * math.pi / L)
    phase = phase.astype(np.float64)
    values = np.where(column % 2 == 0, np.cos(phase), -np.sin(phase))
    values = values.astype(np.float32).astype(jnp.bfloat16).astype(np.float32)
    return (values * np.float32(L ** (-0.5))).astype(jnp.bfloat16)


def exchange_kernel(
    tm_n, chan_n, early, scale, volt, taper, table, late, done, vbuf, wide, filt, mid, send,
    soon, right, made, hist_sem, load_sem, own_sem, send_sem, recv_sem, made_sem,
):
    inputs = volt.shape[0]
    rows = 2 * CH // (tm_n * chan_n)
    steps = SPEC_DEV // STEP
    tm = lax.axis_index("tm")
    chan = lax.axis_index("chan")
    peers = tm_n * chan_n
    me = tm * chan_n + chan
    spread = chan_n // 2 + 2 * tm

    def load_hist():
        part = pl.ds(0, (TAPS - 1) * L)
        return pltpu.make_async_copy(volt.at[:, part], vbuf.at[:, part], hist_sem)

    def load_step(k):
        start = pl.multiple_of((TAPS - 1 + STEP * k) * L, L)
        part = pl.ds(start, STEP * L)
        return pltpu.make_async_copy(volt.at[:, part], vbuf.at[:, part], load_sem.at[k])

    load_hist().start()
    load_step(0).start()

    def partner(j):
        t = lax.rem(tm + j // chan_n, tm_n)
        c = lax.rem(chan + lax.rem(j, chan_n), chan_n)
        return t, c

    barrier = pltpu.get_barrier_semaphore()

    @pl.loop(1, peers)
    def _(j):
        t, c = partner(j)
        pl.semaphore_signal(barrier, inc=1, device_id=(t, c), device_id_type=MESH)

    for p in range(TAPS):
        wide[p] = jnp.broadcast_to(taper[p : p + 1, :], (16, L))

    load_hist().wait()
    lanes = 256

    @pl.loop(0, steps)
    def _(k):
        load_step(k).wait()

        @pl.when(k + 1 < steps)
        def _():
            load_step(k + 1).start()

        @pl.loop(0, STEP // GROUP)
        def _(g):
            first = k * STEP + g * GROUP

            @pl.loop(0, inputs // 16)
            def _(b):
                r0 = pl.multiple_of(b * 16, 16)
                for n0 in range(0, L, lanes):
                    frames = []
                    for f in range(GROUP + TAPS - 1):
                        start = pl.multiple_of((first + f) * L + n0, 128)
                        frames.append(vbuf[pl.ds(r0, 16), pl.ds(start, lanes)].astype(jnp.float32))
                    weights = [wide[p, :, n0 : n0 + lanes] for p in range(TAPS)]
                    for s in range(GROUP):
                        total = weights[0] * frames[s]
                        for p in range(1, TAPS):
                            total = total + weights[p] * frames[s + p]
                        filt[s, pl.ds(r0, 16), n0 : n0 + lanes] = total.astype(jnp.bfloat16)

            for s in range(0, GROUP, 2):
                pair = filt[s : s + 2].reshape(2 * inputs, L)
                for h in range(0, 2 * CH, 256):
                    out = lax.dot_general(
                        table[h : h + 256], pair, (((1,), (1,)), ((), ())),
                        preferred_element_type=jnp.float32,
                    )
                    for q in range(2):
                        row = pl.multiple_of((g * GROUP + s + q) * (2 * CH), 2 * CH)
                        mid[pl.ds(row + h, 256), :] = out[:, q * inputs : (q + 1) * inputs]

        @pl.loop(0, 2 * CH // 8)
        def _(b):
            for u in range(8):
                col = b * 8 + u
                send[k, col] = mid[pl.ds(col, STEP, stride=2 * CH), :].astype(jnp.bfloat16)

        @pl.when(k == 0)
        def _():
            pl.semaphore_wait(barrier, peers - 1)

        @pl.loop(0, peers)
        def _(n):
            j = lax.rem(n + spread, peers)

            @pl.when(j != 0)
            def _():
                t, c = partner(j)
                pltpu.make_async_remote_copy(
                    src_ref=send.at[k, pl.ds((t * chan_n + c) * rows, early)],
                    dst_ref=soon.at[me, k],
                    send_sem=send_sem.at[0, j],
                    recv_sem=recv_sem.at[0, j],
                    device_id=(t, c),
                    device_id_type=MESH,
                ).start()

    own_soon = pltpu.make_async_copy(
        send.at[:, pl.ds(me * rows, early)], soon.at[me], own_sem.at[0]
    )
    own_late = pltpu.make_async_copy(
        send.at[:, pl.ds(me * rows + early, rows - early)], late.at[me], own_sem.at[1]
    )
    own_soon.start()
    own_late.start()

    @pl.loop(0, peers)
    def _(n):
        j = lax.rem(n + spread, peers)

        @pl.when(j != 0)
        def _():
            t, c = partner(j)
            pltpu.make_async_remote_copy(
                src_ref=send.at[:, pl.ds((t * chan_n + c) * rows + early, rows - early)],
                dst_ref=late.at[me],
                send_sem=send_sem.at[1, j],
                recv_sem=recv_sem.at[1, j],
                device_id=(t, c),
                device_id_type=MESH,
            ).start()

    def finish(part, land):
        @pl.loop(1, peers)
        def _(j):
            t, c = partner(j)
            source = lax.rem(tm + tm_n - j // chan_n, tm_n) * chan_n + lax.rem(
                chan + chan_n - lax.rem(j, chan_n), chan_n
            )
            whole = pltpu.make_async_remote_copy(
                src_ref=land.at[source],
                dst_ref=land.at[source],
                send_sem=send_sem.at[part, j],
                recv_sem=recv_sem.at[part, j],
                device_id=(t, c),
                device_id_type=MESH,
            )
            whole.wait_send()
            whole.wait_recv()

    own_soon.wait()
    finish(0, soon)

    @pl.loop(0, early // 2)
    def _(c):
        gather_rows(chan_n, soon, 2 * c, right)
        for m in range(0, right.shape[1], TILE):
            made[:, m : m + TILE] = correlate_tile(right, m, scale)
        written = pltpu.make_async_copy(made, done.at[c], made_sem)
        written.start()
        written.wait()

    own_late.wait()
    finish(1, late)


TILE = 256


def gather_rows(chan_n, spec, row, right):
    peers, steps, _, step, inputs = spec.shape
    depth = right.shape[0] // 2
    for p in range(peers):
        t, g = p // chan_n, p % chan_n
        for k in range(steps):
            for r in range(2):
                first = r * depth + (t * steps + k) * step
                right[first : first + step, g * inputs : (g + 1) * inputs] = spec[p, k, row + r]


def correlate_tile(right, m, scale):
    depth = right.shape[0] // 2
    turned = right[:, m : m + TILE].T
    other = jnp.concatenate([turned[:, depth:], -turned[:, :depth]], axis=1)
    both = jnp.concatenate([turned, other], axis=0)
    block = lax.dot_general(
        both, right[...], (((1,), (0,)), ((), ())), preferred_element_type=jnp.float32
    )
    return (block * scale).astype(jnp.bfloat16).reshape(2, TILE, right.shape[1])


def exchange(voltages, taper_weights, tm_n, chan_n):
    inputs = voltages.shape[0]
    rows = 2 * CH // (tm_n * chan_n)
    steps = SPEC_DEV // STEP
    peers = tm_n * chan_n
    depth = SPEC_DEV * tm_n
    count = inputs * chan_n
    early = 2 * (3 * rows // 16)
    table = jnp.asarray(table_rows())
    return pl.pallas_call(
        functools.partial(exchange_kernel, tm_n, chan_n, early, 1.0 / depth),
        out_shape=(
            jax.ShapeDtypeStruct((peers, steps, rows - early, STEP, inputs), jnp.bfloat16),
            jax.ShapeDtypeStruct((early // 2, 2, count, count), jnp.bfloat16),
        ),
        in_specs=[
            pl.BlockSpec(memory_space=pl.ANY),
            pl.BlockSpec(memory_space=pltpu.VMEM),
            pl.BlockSpec(memory_space=pltpu.VMEM),
        ],
        out_specs=(pl.BlockSpec(memory_space=pl.ANY), pl.BlockSpec(memory_space=pl.ANY)),
        scratch_shapes=[
            pltpu.VMEM(voltages.shape, jnp.bfloat16),
            pltpu.VMEM((TAPS, 16, L), jnp.float32),
            pltpu.VMEM((GROUP, inputs, L), jnp.bfloat16),
            pltpu.VMEM((STEP * 2 * CH, inputs), jnp.float32),
            pltpu.VMEM((steps, 2 * CH, STEP, inputs), jnp.bfloat16),
            pltpu.VMEM((peers, steps, early, STEP, inputs), jnp.bfloat16),
            pltpu.VMEM((2 * depth, count), jnp.bfloat16),
            pltpu.VMEM((2, count, count), jnp.bfloat16),
            pltpu.SemaphoreType.DMA,
            pltpu.SemaphoreType.DMA((steps,)),
            pltpu.SemaphoreType.DMA((2,)),
            pltpu.SemaphoreType.DMA((2, peers)),
            pltpu.SemaphoreType.DMA((2, peers)),
            pltpu.SemaphoreType.DMA,
        ],
        compiler_params=pltpu.CompilerParams(
            collective_id=0, has_side_effects=True, vmem_limit_bytes=60 * MIB
        ),
        cost_estimate=pl.CostEstimate(
            flops=4 * CH * L * inputs * SPEC_DEV, bytes_accessed=40 * MIB, transcendentals=0
        ),
    )(voltages, taper_weights, table)


def correlate_kernel(chan_n, scale, spec, done, out, right, made, done_sem, made_sem):
    c = pl.program_id(0)
    last = pl.num_programs(0) - 1
    ready = done.shape[0]
    tiles = right.shape[1] // TILE

    def hand_on(d):
        return pltpu.make_async_copy(done.at[d], out.at[d], done_sem.at[d])

    def write(channel, i):
        slot = lax.rem(channel, 2)
        part = pl.ds(i * TILE, TILE)
        return pltpu.make_async_copy(
            made.at[slot, :, part], out.at[ready + channel, :, part], made_sem.at[slot, i]
        )

    @pl.when(c == 0)
    def _():
        for d in range(ready):
            hand_on(d).start()

    gather_rows(chan_n, spec, 0, right)
    for i in range(tiles):
        @pl.when(c >= 2)
        def _():
            write(c - 2, i).wait()

        made[lax.rem(c, 2), :, i * TILE : (i + 1) * TILE] = correlate_tile(right, i * TILE, scale)
        write(c, i).start()

    @pl.when(c == last)
    def _():
        for i in range(tiles):
            @pl.when(c >= 1)
            def _():
                write(c - 1, i).wait()

            write(c, i).wait()
        for d in range(ready):
            hand_on(d).wait()


def correlate_all(spectra, done, chan_n):
    peers, steps, rows, step, inputs = spectra.shape
    channels = rows // 2
    ready = done.shape[0]
    depth = peers // chan_n * steps * step
    count = chan_n * inputs
    return pl.pallas_call(
        functools.partial(correlate_kernel, chan_n, 1.0 / depth),
        grid=(channels,),
        out_shape=jax.ShapeDtypeStruct((ready + channels, 2, count, count), jnp.bfloat16),
        in_specs=[
            pl.BlockSpec((peers, steps, 2, step, inputs), lambda c: (0, 0, c, 0, 0)),
            pl.BlockSpec(memory_space=pl.ANY),
        ],
        out_specs=pl.BlockSpec(memory_space=pl.ANY),
        scratch_shapes=[
            pltpu.VMEM((2 * depth, count), jnp.bfloat16),
            pltpu.VMEM((2, 2, count, count), jnp.bfloat16),
            pltpu.SemaphoreType.DMA((ready,)),
            pltpu.SemaphoreType.DMA((2, count // TILE)),
        ],
        compiler_params=pltpu.CompilerParams(vmem_limit_bytes=60 * MIB),
        cost_estimate=pl.CostEstimate(
            flops=8 * channels * count * count * depth,
            bytes_accessed=channels * count * (4 * count + 4 * depth),
            transcendentals=0,
        ),
    )(spectra, done)


def dft_table(length, channels):
    sample_idx = jnp.arange(length, dtype=jnp.int32)[:, None]
    column = jnp.arange(2 * channels, dtype=jnp.int32)[None, :]
    freq = column // 2 + channels // 2
    phase = (sample_idx * freq % length).astype(jnp.float32) * (2.0 * math.pi / length)
    values = jnp.where(column % 2 == 0, jnp.cos(phase), -jnp.sin(phase))
    return values.astype(jnp.bfloat16)


def contract(rows, cols):
    return lax.dot_general(rows, cols, (((1,), (1,)), ((), ())), preferred_element_type=jnp.float32)


def correlate(spec):
    real_part = spec[0]
    imag_part = spec[1]
    left_rows = jnp.concatenate([real_part, imag_part], axis=1)
    other_rows = jnp.concatenate([imag_part, -real_part], axis=1)
    count = left_rows.shape[0]
    stacked = jnp.concatenate([left_rows, other_rows], axis=0)
    return contract(stacked, left_rows).reshape(2, count, count)


def shards_narrow(voltages, taper_weights, time_count, chan_count):
    inputs_here = voltages.shape[0]
    frame_count = SPEC_DEV + TAPS - 1
    frames = voltages.reshape(inputs_here, frame_count, L)
    filtered = taper_weights[0][None, None, :] * frames[:, 0:SPEC_DEV, :].astype(jnp.float32)
    for tap_index in range(1, TAPS):
        filtered = filtered + taper_weights[tap_index][None, None, :] * frames[
            :, tap_index : tap_index + SPEC_DEV, :
        ].astype(jnp.float32)
    filtered = filtered.astype(jnp.bfloat16)
    table = dft_table(L, CH)
    spectra = jnp.einsum(
        "isn,nc->cis", filtered, table, preferred_element_type=jnp.float32
    ) * L ** (-0.5)
    spectra = spectra.astype(jnp.bfloat16)
    per_owner = CH // (time_count * chan_count)
    spectra = spectra.reshape(time_count, chan_count, per_owner, 2, inputs_here, SPEC_DEV)
    scale = 1.0 / (SPEC_DEV * time_count)
    turned = lax.all_to_all(spectra, "tm", split_axis=0, concat_axis=5, tiled=True)
    piece = lax.all_to_all(turned, "chan", split_axis=1, concat_axis=4, tiled=True)
    flat = piece.reshape(piece.shape[2], 2, piece.shape[4], piece.shape[5])
    visibilities = lax.map(correlate, flat) * scale
    return visibilities.astype(jnp.bfloat16)


def shards(voltages, taper_weights):
    time_count = lax.axis_size("tm")
    chan_count = lax.axis_size("chan")
    if voltages.shape[0] % 128 == 0:
        late, done = exchange(voltages, taper_weights, time_count, chan_count)
        return correlate_all(late, done, chan_count)
    return shards_narrow(voltages, taper_weights, time_count, chan_count)


def solution(mesh):
    placed = (P("chan", "tm"), P())
    return jax.shard_map(
        shards,
        mesh=mesh,
        in_specs=placed,
        out_specs=P(("tm", "chan"), None, None, None),
        check_vma=False,
    )
```

```python
import functools
import math

import jax
import jax.numpy as jnp
import numpy as np
from jax import lax
from jax.experimental import pallas as pl
from jax.experimental.pallas import tpu as pltpu
from jax.sharding import PartitionSpec as P

L = 1024
CH = 256
TAPS = 4
SPEC_DEV = 64
MIB = 1024 * 1024
MESH = pl.DeviceIdType.MESH

STEP = 16
GROUP = 4


def table_rows():
    sample_idx = np.arange(L, dtype=np.int64)[None, :]
    column = np.arange(2 * CH, dtype=np.int64)[:, None]
    freq = column // 2 + CH // 2
    phase = (sample_idx * freq % L).astype(np.float32) * np.float32(2.0 * math.pi / L)
    phase = phase.astype(np.float64)
    values = np.where(column % 2 == 0, np.cos(phase), -np.sin(phase))
    values = values.astype(np.float32).astype(jnp.bfloat16).astype(np.float32)
    return (values * np.float32(L ** (-0.5))).astype(jnp.bfloat16)


def exchange_kernel(
    tm_n, chan_n, early, scale, volt, taper, table, late, done, vbuf, wide, filt, mid, send,
    soon, right, made, hist_sem, load_sem, own_sem, send_sem, recv_sem, made_sem,
):
    inputs = volt.shape[0]
    rows = 2 * CH // (tm_n * chan_n)
    steps = SPEC_DEV // STEP
    tm = lax.axis_index("tm")
    chan = lax.axis_index("chan")
    peers = tm_n * chan_n
    me = tm * chan_n + chan

    def load_hist():
        part = pl.ds(0, (TAPS - 1) * L)
        return pltpu.make_async_copy(volt.at[:, part], vbuf.at[:, part], hist_sem)

    def load_step(k):
        start = pl.multiple_of((TAPS - 1 + STEP * k) * L, L)
        part = pl.ds(start, STEP * L)
        return pltpu.make_async_copy(volt.at[:, part], vbuf.at[:, part], load_sem.at[k])

    load_hist().start()
    load_step(0).start()

    def partner(j):
        t = lax.rem(tm + j // chan_n, tm_n)
        c = lax.rem(chan + lax.rem(j, chan_n), chan_n)
        return t, c

    def order(n):
        half = chan_n // 2
        far = lax.rem(n, 2) * half + lax.rem(n, chan_n) // 2
        return n // chan_n * chan_n + lax.rem(far + 2 * tm, chan_n)

    barrier = pltpu.get_barrier_semaphore()

    @pl.loop(1, peers)
    def _(j):
        t, c = partner(j)
        pl.semaphore_signal(barrier, inc=1, device_id=(t, c), device_id_type=MESH)

    for p in range(TAPS):
        wide[p] = jnp.broadcast_to(taper[p : p + 1, :], (16, L))

    load_hist().wait()
    lanes = 256

    @pl.loop(0, steps)
    def _(k):
        load_step(k).wait()

        @pl.when(k + 1 < steps)
        def _():
            load_step(k + 1).start()

        @pl.loop(0, STEP // GROUP)
        def _(g):
            first = k * STEP + g * GROUP

            @pl.loop(0, inputs // 16)
            def _(b):
                r0 = pl.multiple_of(b * 16, 16)
                for n0 in range(0, L, lanes):
                    frames = []
                    for f in range(GROUP + TAPS - 1):
                        start = pl.multiple_of((first + f) * L + n0, 128)
                        frames.append(vbuf[pl.ds(r0, 16), pl.ds(start, lanes)].astype(jnp.float32))
                    weights = [wide[p, :, n0 : n0 + lanes] for p in range(TAPS)]
                    for s in range(GROUP):
                        total = weights[0] * frames[s]
                        for p in range(1, TAPS):
                            total = total + weights[p] * frames[s + p]
                        filt[s, pl.ds(r0, 16), n0 : n0 + lanes] = total.astype(jnp.bfloat16)

            for s in range(0, GROUP, 2):
                pair = filt[s : s + 2].reshape(2 * inputs, L)
                for h in range(0, 2 * CH, 256):
                    out = lax.dot_general(
                        table[h : h + 256], pair, (((1,), (1,)), ((), ())),
                        preferred_element_type=jnp.float32,
                    )
                    for q in range(2):
                        row = pl.multiple_of((g * GROUP + s + q) * (2 * CH), 2 * CH)
                        mid[pl.ds(row + h, 256), :] = out[:, q * inputs : (q + 1) * inputs]

        @pl.loop(0, 2 * CH // 8)
        def _(b):
            for u in range(8):
                col = b * 8 + u
                send[k, col] = mid[pl.ds(col, STEP, stride=2 * CH), :].astype(jnp.bfloat16)

        @pl.when(k == 0)
        def _():
            pl.semaphore_wait(barrier, peers - 1)

        @pl.loop(0, peers)
        def _(n):
            j = order(n)

            @pl.when(j != 0)
            def _():
                t, c = partner(j)
                pltpu.make_async_remote_copy(
                    src_ref=send.at[k, pl.ds((t * chan_n + c) * rows, early)],
                    dst_ref=soon.at[me, k],
                    send_sem=send_sem.at[0, j],
                    recv_sem=recv_sem.at[0, j],
                    device_id=(t, c),
                    device_id_type=MESH,
                ).start()

    own_soon = pltpu.make_async_copy(
        send.at[:, pl.ds(me * rows, early)], soon.at[me], own_sem.at[0]
    )
    own_late = pltpu.make_async_copy(
        send.at[:, pl.ds(me * rows + early, rows - early)], late.at[me], own_sem.at[1]
    )
    own_soon.start()
    own_late.start()

    @pl.loop(0, peers)
    def _(n):
        j = order(n)

        @pl.when(j != 0)
        def _():
            t, c = partner(j)
            pltpu.make_async_remote_copy(
                src_ref=send.at[:, pl.ds((t * chan_n + c) * rows + early, rows - early)],
                dst_ref=late.at[me],
                send_sem=send_sem.at[1, j],
                recv_sem=recv_sem.at[1, j],
                device_id=(t, c),
                device_id_type=MESH,
            ).start()

    def finish(part, land):
        @pl.loop(1, peers)
        def _(j):
            t, c = partner(j)
            source = lax.rem(tm + tm_n - j // chan_n, tm_n) * chan_n + lax.rem(
                chan + chan_n - lax.rem(j, chan_n), chan_n
            )
            whole = pltpu.make_async_remote_copy(
                src_ref=land.at[source],
                dst_ref=land.at[source],
                send_sem=send_sem.at[part, j],
                recv_sem=recv_sem.at[part, j],
                device_id=(t, c),
                device_id_type=MESH,
            )
            whole.wait_send()
            whole.wait_recv()

    own_soon.wait()
    finish(0, soon)

    @pl.loop(0, early // 2)
    def _(c):
        gather_rows(chan_n, soon, 2 * c, right)
        for m in range(0, right.shape[1], TILE):
            made[:, m : m + TILE] = correlate_tile(right, m, scale)
        written = pltpu.make_async_copy(made, done.at[c], made_sem)
        written.start()
        written.wait()

    own_late.wait()
    finish(1, late)


TILE = 256


def gather_rows(chan_n, spec, row, right):
    peers, steps, _, step, inputs = spec.shape
    depth = right.shape[0] // 2
    for p in range(peers):
        t, g = p // chan_n, p % chan_n
        for k in range(steps):
            for r in range(2):
                first = r * depth + (t * steps + k) * step
                right[first : first + step, g * inputs : (g + 1) * inputs] = spec[p, k, row + r]


def correlate_tile(right, m, scale):
    depth = right.shape[0] // 2
    turned = right[:, m : m + TILE].T
    other = jnp.concatenate([turned[:, depth:], -turned[:, :depth]], axis=1)
    both = jnp.concatenate([turned, other], axis=0)
    block = lax.dot_general(
        both, right[...], (((1,), (0,)), ((), ())), preferred_element_type=jnp.float32
    )
    return (block * scale).astype(jnp.bfloat16).reshape(2, TILE, right.shape[1])


def exchange(voltages, taper_weights, tm_n, chan_n):
    inputs = voltages.shape[0]
    rows = 2 * CH // (tm_n * chan_n)
    steps = SPEC_DEV // STEP
    peers = tm_n * chan_n
    depth = SPEC_DEV * tm_n
    count = inputs * chan_n
    early = 2 * (3 * rows // 16)
    table = jnp.asarray(table_rows())
    return pl.pallas_call(
        functools.partial(exchange_kernel, tm_n, chan_n, early, 1.0 / depth),
        out_shape=(
            jax.ShapeDtypeStruct((peers, steps, rows - early, STEP, inputs), jnp.bfloat16),
            jax.ShapeDtypeStruct((early // 2, 2, count, count), jnp.bfloat16),
        ),
        in_specs=[
            pl.BlockSpec(memory_space=pl.ANY),
            pl.BlockSpec(memory_space=pltpu.VMEM),
            pl.BlockSpec(memory_space=pltpu.VMEM),
        ],
        out_specs=(pl.BlockSpec(memory_space=pl.ANY), pl.BlockSpec(memory_space=pl.ANY)),
        scratch_shapes=[
            pltpu.VMEM(voltages.shape, jnp.bfloat16),
            pltpu.VMEM((TAPS, 16, L), jnp.float32),
            pltpu.VMEM((GROUP, inputs, L), jnp.bfloat16),
            pltpu.VMEM((STEP * 2 * CH, inputs), jnp.float32),
            pltpu.VMEM((steps, 2 * CH, STEP, inputs), jnp.bfloat16),
            pltpu.VMEM((peers, steps, early, STEP, inputs), jnp.bfloat16),
            pltpu.VMEM((2 * depth, count), jnp.bfloat16),
            pltpu.VMEM((2, count, count), jnp.bfloat16),
            pltpu.SemaphoreType.DMA,
            pltpu.SemaphoreType.DMA((steps,)),
            pltpu.SemaphoreType.DMA((2,)),
            pltpu.SemaphoreType.DMA((2, peers)),
            pltpu.SemaphoreType.DMA((2, peers)),
            pltpu.SemaphoreType.DMA,
        ],
        compiler_params=pltpu.CompilerParams(
            collective_id=0, has_side_effects=True, vmem_limit_bytes=60 * MIB
        ),
        cost_estimate=pl.CostEstimate(
            flops=4 * CH * L * inputs * SPEC_DEV, bytes_accessed=40 * MIB, transcendentals=0
        ),
    )(voltages, taper_weights, table)


def correlate_kernel(chan_n, channels, scale, spec, done, out, right, made, passing, in_sem, out_sem, made_sem):
    c = pl.program_id(0)
    last = channels - 1
    ready = done.shape[0]
    tiles = right.shape[1] // TILE

    def take(d):
        return pltpu.make_async_copy(done.at[d], passing.at[d], in_sem.at[d])

    def hand_on(d):
        return pltpu.make_async_copy(passing.at[d], out.at[d], out_sem.at[d])

    def write(channel, i):
        slot = lax.rem(channel, 2)
        part = pl.ds(i * TILE, TILE)
        return pltpu.make_async_copy(
            made.at[slot, :, part], out.at[ready + channel, :, part], made_sem.at[slot, i]
        )

    @pl.when(c == 0)
    def _():
        for d in range(ready):
            take(d).start()

    for d in range(ready):
        @pl.when(c == min(d + 1, channels - 1))
        def _():
            take(d).wait()
            hand_on(d).start()

    gather_rows(chan_n, spec, 0, right)
    for i in range(tiles):
        @pl.when(c >= 2)
        def _():
            write(c - 2, i).wait()

        made[lax.rem(c, 2), :, i * TILE : (i + 1) * TILE] = correlate_tile(right, i * TILE, scale)
        write(c, i).start()

    @pl.when(c == last)
    def _():
        for i in range(tiles):
            @pl.when(c >= 1)
            def _():
                write(c - 1, i).wait()

            write(c, i).wait()
        for d in range(ready):
            hand_on(d).wait()


def correlate_all(spectra, done, chan_n):
    peers, steps, rows, step, inputs = spectra.shape
    channels = rows // 2
    ready = done.shape[0]
    depth = peers // chan_n * steps * step
    count = chan_n * inputs
    return pl.pallas_call(
        functools.partial(correlate_kernel, chan_n, channels, 1.0 / depth),
        grid=(channels,),
        out_shape=jax.ShapeDtypeStruct((ready + channels, 2, count, count), jnp.bfloat16),
        in_specs=[
            pl.BlockSpec((peers, steps, 2, step, inputs), lambda c: (0, 0, c, 0, 0)),
            pl.BlockSpec(memory_space=pl.ANY),
        ],
        out_specs=pl.BlockSpec(memory_space=pl.ANY),
        scratch_shapes=[
            pltpu.VMEM((2 * depth, count), jnp.bfloat16),
            pltpu.VMEM((2, 2, count, count), jnp.bfloat16),
            pltpu.VMEM((ready, 2, count, count), jnp.bfloat16),
            pltpu.SemaphoreType.DMA((ready,)),
            pltpu.SemaphoreType.DMA((ready,)),
            pltpu.SemaphoreType.DMA((2, count // TILE)),
        ],
        compiler_params=pltpu.CompilerParams(vmem_limit_bytes=60 * MIB),
        cost_estimate=pl.CostEstimate(
            flops=8 * channels * count * count * depth,
            bytes_accessed=channels * count * (4 * count + 4 * depth),
            transcendentals=0,
        ),
    )(spectra, done)


def dft_table(length, channels):
    sample_idx = jnp.arange(length, dtype=jnp.int32)[:, None]
    column = jnp.arange(2 * channels, dtype=jnp.int32)[None, :]
    freq = column // 2 + channels // 2
    phase = (sample_idx * freq % length).astype(jnp.float32) * (2.0 * math.pi / length)
    values = jnp.where(column % 2 == 0, jnp.cos(phase), -jnp.sin(phase))
    return values.astype(jnp.bfloat16)


def contract(rows, cols):
    return lax.dot_general(rows, cols, (((1,), (1,)), ((), ())), preferred_element_type=jnp.float32)


def correlate(spec):
    real_part = spec[0]
    imag_part = spec[1]
    left_rows = jnp.concatenate([real_part, imag_part], axis=1)
    other_rows = jnp.concatenate([imag_part, -real_part], axis=1)
    count = left_rows.shape[0]
    stacked = jnp.concatenate([left_rows, other_rows], axis=0)
    return contract(stacked, left_rows).reshape(2, count, count)


def shards_narrow(voltages, taper_weights, time_count, chan_count):
    inputs_here = voltages.shape[0]
    frame_count = SPEC_DEV + TAPS - 1
    frames = voltages.reshape(inputs_here, frame_count, L)
    filtered = taper_weights[0][None, None, :] * frames[:, 0:SPEC_DEV, :].astype(jnp.float32)
    for tap_index in range(1, TAPS):
        filtered = filtered + taper_weights[tap_index][None, None, :] * frames[
            :, tap_index : tap_index + SPEC_DEV, :
        ].astype(jnp.float32)
    filtered = filtered.astype(jnp.bfloat16)
    table = dft_table(L, CH)
    spectra = jnp.einsum(
        "isn,nc->cis", filtered, table, preferred_element_type=jnp.float32
    ) * L ** (-0.5)
    spectra = spectra.astype(jnp.bfloat16)
    per_owner = CH // (time_count * chan_count)
    spectra = spectra.reshape(time_count, chan_count, per_owner, 2, inputs_here, SPEC_DEV)
    scale = 1.0 / (SPEC_DEV * time_count)
    turned = lax.all_to_all(spectra, "tm", split_axis=0, concat_axis=5, tiled=True)
    piece = lax.all_to_all(turned, "chan", split_axis=1, concat_axis=4, tiled=True)
    flat = piece.reshape(piece.shape[2], 2, piece.shape[4], piece.shape[5])
    visibilities = lax.map(correlate, flat) * scale
    return visibilities.astype(jnp.bfloat16)


def shards(voltages, taper_weights):
    time_count = lax.axis_size("tm")
    chan_count = lax.axis_size("chan")
    if voltages.shape[0] % 128 == 0:
        late, done = exchange(voltages, taper_weights, time_count, chan_count)
        return correlate_all(late, done, chan_count)
    return shards_narrow(voltages, taper_weights, time_count, chan_count)


def solution(mesh):
    placed = (P("chan", "tm"), P())
    return jax.shard_map(
        shards,
        mesh=mesh,
        in_specs=placed,
        out_specs=P(("tm", "chan"), None, None, None),
        check_vma=False,
    )
```

```python
import functools
import math

import jax
import jax.numpy as jnp
import numpy as np
from jax import lax
from jax.experimental import pallas as pl
from jax.experimental.pallas import tpu as pltpu
from jax.sharding import PartitionSpec as P

L = 1024
CH = 256
TAPS = 4
SPEC_DEV = 64
MIB = 1024 * 1024
MESH = pl.DeviceIdType.MESH

STEP = 16
GROUP = 4


def table_rows():
    sample_idx = np.arange(L, dtype=np.int64)[None, :]
    column = np.arange(2 * CH, dtype=np.int64)[:, None]
    freq = column // 2 + CH // 2
    phase = (sample_idx * freq % L).astype(np.float32) * np.float32(2.0 * math.pi / L)
    phase = phase.astype(np.float64)
    values = np.where(column % 2 == 0, np.cos(phase), -np.sin(phase))
    values = values.astype(np.float32).astype(jnp.bfloat16).astype(np.float32)
    return (values * np.float32(L ** (-0.5))).astype(jnp.bfloat16)


def exchange_kernel(
    tm_n, chan_n, early, scale, volt, taper, table_in, late, done, table, vbuf, wide, filt, mid, send,
    soon, right, made, table_sem, hist_sem, load_sem, own_sem, send_sem, recv_sem, made_sem,
):
    inputs = volt.shape[0]
    rows = 2 * CH // (tm_n * chan_n)
    steps = SPEC_DEV // STEP
    tm = lax.axis_index("tm")
    chan = lax.axis_index("chan")
    peers = tm_n * chan_n
    me = tm * chan_n + chan

    def load_hist():
        part = pl.ds(0, (TAPS - 1) * L)
        return pltpu.make_async_copy(volt.at[:, part], vbuf.at[:, part], hist_sem)

    def load_step(k):
        start = pl.multiple_of((TAPS - 1 + STEP * k) * L, L)
        part = pl.ds(start, STEP * L)
        return pltpu.make_async_copy(volt.at[:, part], vbuf.at[:, part], load_sem.at[k])

    load_table = pltpu.make_async_copy(table_in, table, table_sem)
    load_hist().start()
    load_step(0).start()
    load_table.start()

    def partner(j):
        t = lax.rem(tm + j // chan_n, tm_n)
        c = lax.rem(chan + lax.rem(j, chan_n), chan_n)
        return t, c

    def order(n):
        half = chan_n // 2
        far = lax.rem(n, 2) * half + lax.rem(n, chan_n) // 2
        return n // chan_n * chan_n + lax.rem(far + 2 * tm, chan_n)

    barrier = pltpu.get_barrier_semaphore()

    @pl.loop(1, peers)
    def _(j):
        t, c = partner(j)
        pl.semaphore_signal(barrier, inc=1, device_id=(t, c), device_id_type=MESH)

    for p in range(TAPS):
        wide[p] = jnp.broadcast_to(taper[p : p + 1, :], (16, L))

    load_hist().wait()
    load_table.wait()
    lanes = 256

    @pl.loop(0, steps)
    def _(k):
        load_step(k).wait()

        @pl.when(k + 1 < steps)
        def _():
            load_step(k + 1).start()

        @pl.loop(0, STEP // GROUP)
        def _(g):
            first = k * STEP + g * GROUP

            @pl.loop(0, inputs // 16)
            def _(b):
                r0 = pl.multiple_of(b * 16, 16)
                for n0 in range(0, L, lanes):
                    frames = []
                    for f in range(GROUP + TAPS - 1):
                        start = pl.multiple_of((first + f) * L + n0, 128)
                        frames.append(vbuf[pl.ds(r0, 16), pl.ds(start, lanes)].astype(jnp.float32))
                    weights = [wide[p, :, n0 : n0 + lanes] for p in range(TAPS)]
                    for s in range(GROUP):
                        total = weights[0] * frames[s]
                        for p in range(1, TAPS):
                            total = total + weights[p] * frames[s + p]
                        filt[s, pl.ds(r0, 16), n0 : n0 + lanes] = total.astype(jnp.bfloat16)

            for s in range(0, GROUP, 2):
                pair = filt[s : s + 2].reshape(2 * inputs, L)
                for h in range(0, 2 * CH, 256):
                    out = lax.dot_general(
                        table[h : h + 256], pair, (((1,), (1,)), ((), ())),
                        preferred_element_type=jnp.float32,
                    )
                    for q in range(2):
                        row = pl.multiple_of((g * GROUP + s + q) * (2 * CH), 2 * CH)
                        mid[pl.ds(row + h, 256), :] = out[:, q * inputs : (q + 1) * inputs]

        @pl.loop(0, 2 * CH // 8)
        def _(b):
            for u in range(8):
                col = b * 8 + u
                send[k, col] = mid[pl.ds(col, STEP, stride=2 * CH), :].astype(jnp.bfloat16)

        @pl.when(k == 0)
        def _():
            pl.semaphore_wait(barrier, peers - 1)

        @pl.loop(0, peers)
        def _(n):
            j = order(n)

            @pl.when(j != 0)
            def _():
                t, c = partner(j)
                pltpu.make_async_remote_copy(
                    src_ref=send.at[k, pl.ds((t * chan_n + c) * rows, early)],
                    dst_ref=soon.at[me, k],
                    send_sem=send_sem.at[0, j],
                    recv_sem=recv_sem.at[0, j],
                    device_id=(t, c),
                    device_id_type=MESH,
                ).start()

    own_soon = pltpu.make_async_copy(
        send.at[:, pl.ds(me * rows, early)], soon.at[me], own_sem.at[0]
    )
    own_late = pltpu.make_async_copy(
        send.at[:, pl.ds(me * rows + early, rows - early)], late.at[me], own_sem.at[1]
    )
    own_soon.start()
    own_late.start()

    @pl.loop(0, peers)
    def _(n):
        j = order(n)

        @pl.when(j != 0)
        def _():
            t, c = partner(j)
            pltpu.make_async_remote_copy(
                src_ref=send.at[:, pl.ds((t * chan_n + c) * rows + early, rows - early)],
                dst_ref=late.at[me],
                send_sem=send_sem.at[1, j],
                recv_sem=recv_sem.at[1, j],
                device_id=(t, c),
                device_id_type=MESH,
            ).start()

    def finish(part, land):
        @pl.loop(1, peers)
        def _(j):
            t, c = partner(j)
            source = lax.rem(tm + tm_n - j // chan_n, tm_n) * chan_n + lax.rem(
                chan + chan_n - lax.rem(j, chan_n), chan_n
            )
            whole = pltpu.make_async_remote_copy(
                src_ref=land.at[source],
                dst_ref=land.at[source],
                send_sem=send_sem.at[part, j],
                recv_sem=recv_sem.at[part, j],
                device_id=(t, c),
                device_id_type=MESH,
            )
            whole.wait_send()
            whole.wait_recv()

    own_soon.wait()
    finish(0, soon)

    @pl.loop(0, early // 2)
    def _(c):
        gather_rows(chan_n, soon, 2 * c, right)
        for m in range(0, right.shape[1], TILE):
            made[:, m : m + TILE] = correlate_tile(right, m, scale)
        written = pltpu.make_async_copy(made, done.at[c], made_sem)
        written.start()
        written.wait()

    own_late.wait()
    finish(1, late)


TILE = 256


def gather_rows(chan_n, spec, row, right):
    peers, steps, _, step, inputs = spec.shape
    depth = right.shape[0] // 2
    for p in range(peers):
        t, g = p // chan_n, p % chan_n
        for k in range(steps):
            for r in range(2):
                first = r * depth + (t * steps + k) * step
                right[first : first + step, g * inputs : (g + 1) * inputs] = spec[p, k, row + r]


def correlate_tile(right, m, scale):
    depth = right.shape[0] // 2
    turned = right[:, m : m + TILE].T
    other = jnp.concatenate([turned[:, depth:], -turned[:, :depth]], axis=1)
    both = jnp.concatenate([turned, other], axis=0)
    block = lax.dot_general(
        both, right[...], (((1,), (0,)), ((), ())), preferred_element_type=jnp.float32
    )
    return (block * scale).astype(jnp.bfloat16).reshape(2, TILE, right.shape[1])


def exchange(voltages, taper_weights, tm_n, chan_n):
    inputs = voltages.shape[0]
    rows = 2 * CH // (tm_n * chan_n)
    steps = SPEC_DEV // STEP
    peers = tm_n * chan_n
    depth = SPEC_DEV * tm_n
    count = inputs * chan_n
    early = 2 * (rows // 8)
    table = jnp.asarray(table_rows())
    return pl.pallas_call(
        functools.partial(exchange_kernel, tm_n, chan_n, early, 1.0 / depth),
        out_shape=(
            jax.ShapeDtypeStruct((peers, steps, rows - early, STEP, inputs), jnp.bfloat16),
            jax.ShapeDtypeStruct((early // 2, 2, count, count), jnp.bfloat16),
        ),
        in_specs=[
            pl.BlockSpec(memory_space=pl.ANY),
            pl.BlockSpec(memory_space=pltpu.VMEM),
            pl.BlockSpec(memory_space=pl.ANY),
        ],
        out_specs=(pl.BlockSpec(memory_space=pl.ANY), pl.BlockSpec(memory_space=pl.ANY)),
        scratch_shapes=[
            pltpu.VMEM(table.shape, jnp.bfloat16),
            pltpu.VMEM(voltages.shape, jnp.bfloat16),
            pltpu.VMEM((TAPS, 16, L), jnp.float32),
            pltpu.VMEM((GROUP, inputs, L), jnp.bfloat16),
            pltpu.VMEM((STEP * 2 * CH, inputs), jnp.float32),
            pltpu.VMEM((steps, 2 * CH, STEP, inputs), jnp.bfloat16),
            pltpu.VMEM((peers, steps, early, STEP, inputs), jnp.bfloat16),
            pltpu.VMEM((2 * depth, count), jnp.bfloat16),
            pltpu.VMEM((2, count, count), jnp.bfloat16),
            pltpu.SemaphoreType.DMA,
            pltpu.SemaphoreType.DMA,
            pltpu.SemaphoreType.DMA((steps,)),
            pltpu.SemaphoreType.DMA((2,)),
            pltpu.SemaphoreType.DMA((2, peers)),
            pltpu.SemaphoreType.DMA((2, peers)),
            pltpu.SemaphoreType.DMA,
        ],
        compiler_params=pltpu.CompilerParams(
            collective_id=0, has_side_effects=True, vmem_limit_bytes=60 * MIB
        ),
        cost_estimate=pl.CostEstimate(
            flops=4 * CH * L * inputs * SPEC_DEV, bytes_accessed=40 * MIB, transcendentals=0
        ),
    )(voltages, taper_weights, table)


def correlate_kernel(chan_n, channels, scale, spec, done, out, right, made, passing, in_sem, out_sem, made_sem):
    c = pl.program_id(0)
    last = channels - 1
    ready = done.shape[0]
    tiles = right.shape[1] // TILE

    def take(d):
        return pltpu.make_async_copy(done.at[d], passing.at[d], in_sem.at[d])

    def hand_on(d):
        return pltpu.make_async_copy(passing.at[d], out.at[d], out_sem.at[d])

    def write(channel, i):
        slot = lax.rem(channel, 2)
        part = pl.ds(i * TILE, TILE)
        return pltpu.make_async_copy(
            made.at[slot, :, part], out.at[ready + channel, :, part], made_sem.at[slot, i]
        )

    @pl.when(c == 0)
    def _():
        for d in range(ready):
            take(d).start()

    for d in range(ready):
        @pl.when(c == min(d + 1, channels - 1))
        def _():
            take(d).wait()
            hand_on(d).start()

    gather_rows(chan_n, spec, 0, right)
    for i in range(tiles):
        @pl.when(c >= 2)
        def _():
            write(c - 2, i).wait()

        made[lax.rem(c, 2), :, i * TILE : (i + 1) * TILE] = correlate_tile(right, i * TILE, scale)
        write(c, i).start()

    @pl.when(c == last)
    def _():
        for i in range(tiles):
            @pl.when(c >= 1)
            def _():
                write(c - 1, i).wait()

            write(c, i).wait()
        for d in range(ready):
            hand_on(d).wait()


def correlate_all(spectra, done, chan_n):
    peers, steps, rows, step, inputs = spectra.shape
    channels = rows // 2
    ready = done.shape[0]
    depth = peers // chan_n * steps * step
    count = chan_n * inputs
    return pl.pallas_call(
        functools.partial(correlate_kernel, chan_n, channels, 1.0 / depth),
        grid=(channels,),
        out_shape=jax.ShapeDtypeStruct((ready + channels, 2, count, count), jnp.bfloat16),
        in_specs=[
            pl.BlockSpec((peers, steps, 2, step, inputs), lambda c: (0, 0, c, 0, 0)),
            pl.BlockSpec(memory_space=pl.ANY),
        ],
        out_specs=pl.BlockSpec(memory_space=pl.ANY),
        scratch_shapes=[
            pltpu.VMEM((2 * depth, count), jnp.bfloat16),
            pltpu.VMEM((2, 2, count, count), jnp.bfloat16),
            pltpu.VMEM((ready, 2, count, count), jnp.bfloat16),
            pltpu.SemaphoreType.DMA((ready,)),
            pltpu.SemaphoreType.DMA((ready,)),
            pltpu.SemaphoreType.DMA((2, count // TILE)),
        ],
        compiler_params=pltpu.CompilerParams(vmem_limit_bytes=60 * MIB),
        cost_estimate=pl.CostEstimate(
            flops=8 * channels * count * count * depth,
            bytes_accessed=channels * count * (4 * count + 4 * depth),
            transcendentals=0,
        ),
    )(spectra, done)


def dft_table(length, channels):
    sample_idx = jnp.arange(length, dtype=jnp.int32)[:, None]
    column = jnp.arange(2 * channels, dtype=jnp.int32)[None, :]
    freq = column // 2 + channels // 2
    phase = (sample_idx * freq % length).astype(jnp.float32) * (2.0 * math.pi / length)
    values = jnp.where(column % 2 == 0, jnp.cos(phase), -jnp.sin(phase))
    return values.astype(jnp.bfloat16)


def contract(rows, cols):
    return lax.dot_general(rows, cols, (((1,), (1,)), ((), ())), preferred_element_type=jnp.float32)


def correlate(spec):
    real_part = spec[0]
    imag_part = spec[1]
    left_rows = jnp.concatenate([real_part, imag_part], axis=1)
    other_rows = jnp.concatenate([imag_part, -real_part], axis=1)
    count = left_rows.shape[0]
    stacked = jnp.concatenate([left_rows, other_rows], axis=0)
    return contract(stacked, left_rows).reshape(2, count, count)


def shards_narrow(voltages, taper_weights, time_count, chan_count):
    inputs_here = voltages.shape[0]
    frame_count = SPEC_DEV + TAPS - 1
    frames = voltages.reshape(inputs_here, frame_count, L)
    filtered = taper_weights[0][None, None, :] * frames[:, 0:SPEC_DEV, :].astype(jnp.float32)
    for tap_index in range(1, TAPS):
        filtered = filtered + taper_weights[tap_index][None, None, :] * frames[
            :, tap_index : tap_index + SPEC_DEV, :
        ].astype(jnp.float32)
    filtered = filtered.astype(jnp.bfloat16)
    table = dft_table(L, CH)
    spectra = jnp.einsum(
        "isn,nc->cis", filtered, table, preferred_element_type=jnp.float32
    ) * L ** (-0.5)
    spectra = spectra.astype(jnp.bfloat16)
    per_owner = CH // (time_count * chan_count)
    spectra = spectra.reshape(time_count, chan_count, per_owner, 2, inputs_here, SPEC_DEV)
    scale = 1.0 / (SPEC_DEV * time_count)
    turned = lax.all_to_all(spectra, "tm", split_axis=0, concat_axis=5, tiled=True)
    piece = lax.all_to_all(turned, "chan", split_axis=1, concat_axis=4, tiled=True)
    flat = piece.reshape(piece.shape[2], 2, piece.shape[4], piece.shape[5])
    visibilities = lax.map(correlate, flat) * scale
    return visibilities.astype(jnp.bfloat16)


def shards(voltages, taper_weights):
    time_count = lax.axis_size("tm")
    chan_count = lax.axis_size("chan")
    if voltages.shape[0] % 128 == 0:
        late, done = exchange(voltages, taper_weights, time_count, chan_count)
        return correlate_all(late, done, chan_count)
    return shards_narrow(voltages, taper_weights, time_count, chan_count)


def solution(mesh):
    placed = (P("chan", "tm"), P())
    return jax.shard_map(
        shards,
        mesh=mesh,
        in_specs=placed,
        out_specs=P(("tm", "chan"), None, None, None),
        check_vma=False,
    )
```
